1024 devices in a mesh: owner: 32 (over x, y), replica: 32 (over z, core).
Axes of the slice: x: 4, y: 8, z: 16, core: 2. Of those that a mesh axis runs over, the one named last changes fastest.
Arguments:
- cold_vals: bfloat16 [65536, 768], P('owner'), may hold values from -6 to 6
- cold_scales: float32 [65536, 6], P('owner'), may hold values from 0.25 to 4
- hot_vals: bfloat16 [4096, 768], P('replica'), may hold values from -6 to 6
- hot_scales: float32 [4096, 6], P('replica'), may hold values from 0.25 to 4
- cold_req: int32 [32, 32, 1024], P('owner', 'replica'), may hold values from 0 to 2047
- hot_holder: int32 [32, 32, 256, 1], P('owner', 'replica'), may hold values from 0 to 31; in each aligned block of 256 rows (0 to 255, 256 to 511, ..., all dimensions but the last counted through in order) at most 16 rows name the same one
- hot_slot: int32 [32, 32, 256], P('owner', 'replica'), may hold values from 0 to 127
- self_pos: int32 [32, 32, 256], P('owner', 'replica'), may hold values from 0 to 1279
- nbr_pos: int32 [32, 32, 256, 15], P('owner', 'replica'), may hold values from 0 to 1279
- nbr_count: int32 [32, 32, 256], P('owner', 'replica'), may hold values from 0 to 15
- w_self: bfloat16 [768, 1024], replicated, may hold values from -0.21875 to 0.21875
- w_nbr: bfloat16 [768, 1024], replicated, may hold values from -0.21875 to 0.21875
- bias: float32 [1024], replicated, may hold values from -3 to 3
Outputs:
- hidden: bfloat16 [32, 32, 256, 1024], P('owner', 'replica')
The draws below stay inside these ranges and needn't reach their ends.
Inputs may be any that keep to these rules, and one draw needn't show every extreme that they name: `cold_req`: each device asks every owner for exactly 32 rows. `hot_holder`: at most 16 of one device's requests name one holder.
All inputs are finite; a program needn't handle non-finite values.
Results may differ from the reference program's by a relative error of at most 0.005.
Values may be sent and summed in bfloat16 or wider, within the bound.
No kernel may reach another device: no remote copies, remote signals or barrier semaphores. Data moves between devices by JAX's collectives and lax.ppermute only.
A program may use at most 64 MiB of HBM per device.

```python
import math
import jax
import jax.numpy as jnp
import numpy as np
from jax import lax

D = 768
HID = 1024
F = 15
SB = 128
NB = 6
ROWS_DEV = 2048
CAP = 32
HOT_DEV = 128
HREQ = 256
TGT = 256
HCAP = 16
POOL = 1280
ROWS = 65536
HOT = 4096
N_OWNER = 32
N_REPLICA = 32


def place_ends(entries, own_key, smallest, largest):
    extent = entries.shape
    spot = [jax.random.randint(jax.random.fold_in(own_key, axis), (), 0, extent[axis]) for axis in range(len(extent))]
    entries = entries.at[tuple(spot)].set(smallest)
    longest = extent.index(max(extent))
    spot[longest] = (spot[longest] + 1) % extent[longest]
    return entries.at[tuple(spot)].set(largest)


def shard_levels(own_key, extent, pieces, low, largest):
    gain, own = 1.0, jax.random.fold_in(own_key, 6)
    for position, parts in pieces:
        steps = jnp.exp(jax.random.uniform(jax.random.fold_in(own, position), (parts,), jnp.float32, low / len(pieces), largest / len(pieces)))
        gain = gain * jnp.repeat(steps, extent[position] // parts).reshape([-1 if axis == position else 1 for axis in range(len(extent))])
    return gain


def deal_out(rng, own, number, rows, count, top, limit, skew):
    order = jax.random.permutation(rng, count)
    crowded, usual = portions_of(count, rows * top, limit, skew, True), portions_of(count, rows * top, limit, skew, False)
    places = jnp.arange(count)

    def named(lengths, turn):
        used = int((lengths > 0).sum())
        fixed = max(1, used // 4)
        passed = fixed + (places - fixed + turn * (used - fixed)) % max(1, count - fixed)
        return jnp.zeros((count,), jnp.int32).at[order[jnp.where(places < fixed, places, passed)]].set(jnp.asarray(lengths, jnp.int32))

    lengths = jnp.where(number % 4 == 0, named(crowded, number // 4), named(usual, number - number // 4 - 1))
    mixed = jax.random.permutation(jax.random.fold_in(own, 3), count)
    giver, taker = mixed[0:count // 2 * 2:2], mixed[1:count // 2 * 2:2]
    margin = jnp.minimum(lengths[giver] - 1, limit - lengths[taker]) // 2
    margin = jnp.where((giver == order[0]) | (taker == order[0]) | (lengths[taker] == 0), 0, jnp.maximum(margin, 0))
    passed = jax.random.randint(jax.random.fold_in(own, 4), (count // 2,), 0, 1 << 20) % (margin + 1)
    lengths = lengths.at[giver].add(-passed).at[taker].add(passed)
    labels = jnp.searchsorted(jnp.cumsum(lengths), jnp.arange(rows * top), side="right").astype(jnp.int32)
    table = labels.reshape(top, rows).T
    table = table[jax.random.permutation(jax.random.fold_in(own, 1), rows)]
    turn = jax.random.randint(jax.random.fold_in(own, 2), (rows, 1), 0, top)
    return jnp.take_along_axis(table, (jnp.arange(top)[None, :] + turn) % top, axis=1)


def portions_of(amount, total, bound, lean, full):
    portions = [(1 << 20) // math.isqrt(rank ** lean) + 1 for rank in range(1, amount + 1)]
    largest = bound if full else min(bound, max(-(-total // amount), total * portions[0] // sum(portions)))
    least = 1 if total - largest >= amount - 1 else 0
    given, spare = [largest] + [least] * (amount - 1), total - largest - least * (amount - 1)
    while spare > 0:
        candidates = [i for i in range(1, amount) if given[i] < largest] or [i for i in range(1, amount) if given[i] < bound]
        whole, remaining = sum([portions[i] for i in candidates]), spare
        for i in candidates:
            addition = min(bound - given[i], max(1, remaining * portions[i] // whole), spare)
            given[i] = given[i] + addition
            spare = spare - addition
    return np.array(given)


def noise(stream_key, shape, width, limit, pieces=(), held_as=jnp.bfloat16):
    values = jax.random.normal(stream_key, shape, jnp.float32) * width
    if len(pieces) > 0:
        values = shard_levels(stream_key, shape, pieces, -0.22, 0.18) * values
    return jnp.clip(values, min=-limit, max=limit).astype(held_as)


def setup_inputs(seed: int = 0) -> dict:
    key_of = jax.random.split(jax.random.key(seed), 14)
    cold_vals = noise(key_of[0], (ROWS, D), 1.0, 6.0, ((0, 32),))
    cold_scales = jnp.clip(jnp.exp(math.log(4.0) - 2.7725887 * jax.random.uniform(key_of[1], (ROWS, NB), jnp.float32) ** shard_levels(key_of[1], (ROWS, NB), ((0, 32),), -0.2, 0.2)), 0.25, 4.0)
    hot_vals = noise(key_of[2], (HOT, D), 1.0, 6.0, ((0, 32),))
    hot_scales = jnp.clip(jnp.exp(math.log(4.0) - 2.7725887 * jax.random.uniform(key_of[3], (HOT, NB), jnp.float32) ** shard_levels(key_of[3], (HOT, NB), ((0, 32),), -0.2, 0.2)), 0.25, 4.0)
    cold_req = place_ends(jax.random.randint(key_of[4], (N_OWNER, N_REPLICA, N_OWNER * CAP), 0, ROWS_DEV), jax.random.fold_in(key_of[4], 1), 0, ROWS_DEV - 1).astype(jnp.int32)
    hot_holder_keys = jax.random.split(jax.random.fold_in(key_of[5], 1), N_OWNER * N_REPLICA * HREQ // HREQ)
    hot_holder_turns = jax.random.permutation(jax.random.fold_in(key_of[5], 3), N_OWNER * N_REPLICA * HREQ // HREQ)
    hot_holder = jax.vmap(lambda own, number: deal_out(jax.random.fold_in(key_of[5], 2), own, number, HREQ, N_REPLICA, 1, HCAP, 2))(hot_holder_keys, hot_holder_turns).reshape((N_OWNER, N_REPLICA, HREQ, 1))
    hot_slot = place_ends(jax.random.randint(key_of[6], (N_OWNER, N_REPLICA, HREQ), 0, HOT_DEV), jax.random.fold_in(key_of[6], 1), 0, HOT_DEV - 1).astype(jnp.int32)
    self_pos = place_ends(jax.random.randint(key_of[7], (N_OWNER, N_REPLICA, TGT), 0, POOL), jax.random.fold_in(key_of[7], 1), 0, POOL - 1).astype(jnp.int32)
    nbr_pos = place_ends(jax.random.randint(key_of[8], (N_OWNER, N_REPLICA, TGT, F), 0, POOL), jax.random.fold_in(key_of[8], 1), 0, POOL - 1).astype(jnp.int32)
    nbr_count = place_ends(jax.random.randint(key_of[9], (N_OWNER, N_REPLICA, TGT), 0, F + 1), jax.random.fold_in(key_of[9], 1), 0, F).astype(jnp.int32)
    w_self = noise(key_of[10], (D, HID), D ** -0.5, 0.21875)
    w_nbr = noise(key_of[11], (D, HID), D ** -0.5, 0.21875)
    bias = noise(key_of[12], (HID,), 0.5, 3.0, (), jnp.float32)
    return dict(cold_vals=cold_vals, cold_scales=cold_scales, hot_vals=hot_vals, hot_scales=hot_scales, cold_req=cold_req, hot_holder=hot_holder, hot_slot=hot_slot, self_pos=self_pos, nbr_pos=nbr_pos, nbr_count=nbr_count, w_self=w_self, w_nbr=w_nbr, bias=bias)


def dequantize(values, scales):
    count = values.shape[0]
    blocks = values.astype(jnp.float32).reshape(count, NB, SB) * scales[:, :, None]
    return blocks.reshape(count, D).astype(jnp.bfloat16)


def device_layer(pool, self_rows, neighbours, counts, w_self, w_nbr, bias):
    selfx = pool[self_rows]
    live = (jnp.arange(F, dtype=jnp.int32)[None, :] < counts[:, None]).astype(jnp.float32)
    gathered = pool[neighbours].astype(jnp.float32)
    total = jnp.sum(gathered * live[:, :, None], axis=1)
    nbr_mean = (total / jnp.maximum(counts, 1).astype(jnp.float32)[:, None]).astype(jnp.bfloat16)
    mixed = jnp.dot(selfx, w_self, preferred_element_type=jnp.float32)
    mixed = mixed + jnp.dot(nbr_mean, w_nbr, preferred_element_type=jnp.float32) + bias[None, :]
    return jnp.maximum(mixed, 0.0).astype(jnp.bfloat16)


def reference(cold_vals, cold_scales, hot_vals, hot_scales, cold_req, hot_holder, hot_slot, self_pos, nbr_pos, nbr_count, w_self, w_nbr, bias):
    offsets = jnp.repeat(jnp.arange(N_OWNER, dtype=jnp.int32) * ROWS_DEV, CAP)

    def per_owner(owner_index):
        asks = cold_req[owner_index] + offsets[None, :]
        flat = asks.reshape(-1)
        cold_rows = dequantize(cold_vals[flat], cold_scales[flat]).reshape(N_REPLICA, N_OWNER * CAP, D)
        wanted = (hot_holder[owner_index][:, :, 0] * HOT_DEV + hot_slot[owner_index]).reshape(-1)
        hot_rows = dequantize(hot_vals[wanted], hot_scales[wanted]).reshape(N_REPLICA, HREQ, D)
        pool = jnp.concatenate([cold_rows, hot_rows], axis=1)
        layer = jax.vmap(device_layer, in_axes=(0, 0, 0, 0, None, None, None))
        return layer(pool, self_pos[owner_index], nbr_pos[owner_index], nbr_count[owner_index], w_self, w_nbr, bias)

    return lax.map(per_owner, jnp.arange(N_OWNER, dtype=jnp.int32))
```

```python
import jax
import jax.numpy as jnp
from jax import lax
from jax.experimental import pallas as pl
from jax.experimental.pallas import tpu as pltpu
from jax.sharding import PartitionSpec as P

D = 768
F = 15
SB = 128
NB = 6
HCAP = 16
LANES = 128
MIB = 1024 * 1024
F32 = jnp.float32
BF16 = jnp.bfloat16
I32 = jnp.int32


def iota(shape, axis):
    return lax.broadcasted_iota(I32, shape, axis)


def call(body, outs, ins, scalars=0, scratch=(), vmem=16, flops=0, moved=0):
    smem = pl.BlockSpec(memory_space=pltpu.SMEM)
    full = pl.BlockSpec(memory_space=pltpu.VMEM)
    many = isinstance(outs, (list, tuple))
    return pl.pallas_call(
        body,
        out_shape=outs,
        in_specs=[smem] * scalars + [full] * (len(ins) - scalars),
        out_specs=[full] * len(outs) if many else full,
        scratch_shapes=list(scratch),
        compiler_params=pltpu.CompilerParams(vmem_limit_bytes=vmem * MIB),
        cost_estimate=pl.CostEstimate(flops=flops, bytes_accessed=moved, transcendentals=0),
    )(*ins)


def dequantize_kernel(vals_ref, scales_ref, out_ref):
    def chunk(at, carry):
        rows = pl.ds(pl.multiple_of(at * LANES, LANES), LANES)
        across = scales_ref[:, rows]
        square = jnp.concatenate([across, jnp.zeros((LANES - NB, LANES), F32)], axis=0)
        down = square.T
        for block in range(NB):
            cols = slice(block * SB, (block + 1) * SB)
            out_ref[rows, cols] = (
                vals_ref[rows, cols].astype(F32) * down[:, block : block + 1]
            ).astype(BF16)
        return carry

    lax.fori_loop(0, vals_ref.shape[0] // LANES, chunk, 0)


def dequantize(vals, scales):
    rows = vals.shape[0]
    return call(
        dequantize_kernel,
        jax.ShapeDtypeStruct((rows, D), BF16),
        [vals, scales.T],
        vmem=12,
        flops=rows * D,
        moved=rows * D * 4,
    )


def server_of(holder):
    return (holder // 2) % 8


def local_of(holder, core):
    return (holder // 16) * 2 + jnp.bitwise_xor(holder % 2, core)


def ask_kernel(core_ref, cold_ref, holder_ref, slot_ref, ask_ref, place_ref):
    core = core_ref[0]
    n = holder_ref.shape[1]
    across = jnp.broadcast_to(holder_ref[...], (n, n))
    down = across.T
    earlier = (across == down) & (iota((n, n), 1) < iota((n, n), 0))
    rank = jnp.sum(earlier.astype(F32), axis=1, keepdims=True).astype(I32)
    down = down[:, :LANES]
    lane = local_of(down, core) * HCAP + rank
    place_ref[...] = server_of(down) * 64 + lane
    owners = ask_ref.shape[0]
    server = iota((owners, n), 0)
    server = (server // 8) * 2 + server % 2
    named = server_of(jnp.broadcast_to(holder_ref[...], (owners, n))) == server
    slots = jnp.broadcast_to(slot_ref[...], (owners, n)).astype(F32)
    left = jnp.where(named, slots, 0.0).astype(BF16)
    right = (lane + 32 == iota((n, LANES), 1)).astype(F32).astype(BF16)
    hot = jnp.dot(left, right, preferred_element_type=F32).astype(I32)
    column = iota((1, LANES), 1)
    base = jnp.clip((column - 32) // HCAP, 0, 3) * LANES
    for p in range(owners):
        cold = cold_ref[:, (p // 4) * LANES : (p // 4 + 1) * LANES]
        if p % 4:
            cold = pltpu.roll(cold, LANES - 32 * (p % 4), 1)
        ask_ref[p] = jnp.where(column < 32, cold, hot[p : p + 1] + base)


def transposed(rows):
    n = rows.shape[0]
    if n < LANES:
        rows = jnp.concatenate([rows, jnp.zeros((LANES - n, LANES), I32)], axis=0)
    return rows.T


def serve_cold_kernel(asked_ref, table_ref, out_ref):
    asks = transposed(jnp.concatenate([asked_ref[p] for p in range(32)], axis=0))
    rows = table_ref.shape[0]
    group = 8
    for first in range(0, 32, group):
        mask = jnp.concatenate(
            [
                (asks[:32, p : p + 1] == iota((32, rows), 1)).astype(F32).astype(BF16)
                for p in range(first, first + group)
            ],
            axis=0,
        )
        out_ref[first * 32 : (first + group) * 32, :] = jnp.dot(
            mask, table_ref[...], preferred_element_type=F32
        ).astype(BF16)


def serve_hot_kernel(pair_ref, asked_ref, u_ref, u2_ref, d_ref, d2_ref, out_ref):
    pair = pair_ref[0]
    asks = transposed(
        jnp.concatenate([asked_ref[x * 8 + 2 * pair + b] for x in range(4) for b in range(2)], axis=0)
    )
    for q in range(8):
        for piece, ref in enumerate((u_ref, u2_ref, d_ref, d2_ref)):
            at = 32 + piece * HCAP
            mask = asks[at : at + HCAP, q : q + 1] == iota((HCAP, LANES), 1) + piece * LANES
            out_ref[q * 64 + piece * HCAP : q * 64 + (piece + 1) * HCAP, :] = jnp.dot(
                mask.astype(F32).astype(BF16), ref[...], preferred_element_type=F32
            ).astype(BF16)


def weigh_kernel(self_ref, nbr_ref, count_ref, place_ref, cold_ref, hot_ref, divisor_ref):
    n = self_ref.shape[1]
    count = count_ref[...]
    own = self_ref[...]
    live = [jnp.where(count > f, nbr_ref[f], -1) for f in range(F)]

    def chunk(at):
        position = iota((LANES, n), 0) + at * LANES
        picked = (own == position).astype(F32)
        times = jnp.zeros((LANES, n), F32)
        for f in range(F):
            times = times + (live[f] == position).astype(F32)
        return picked.T.astype(BF16), times.T.astype(BF16)

    n_cold = cold_ref.shape[1] // LANES
    for at in range(n_cold):
        picked, times = chunk(at)
        cols = slice(at * LANES, (at + 1) * LANES)
        cold_ref[:n, cols] = picked
        cold_ref[n:, cols] = times
    slots = hot_ref.shape[1]
    pieces = []
    for at in range(place_ref.shape[0] // LANES):
        picked, times = chunk(n_cold + at)
        place = place_ref[at * LANES : (at + 1) * LANES, :]
        place = jnp.concatenate([place] * (slots // LANES), axis=1)
        spread = (place == iota((LANES, slots), 1)).astype(F32).astype(BF16)
        both = jnp.concatenate([picked, times], axis=0)
        pieces.append(jnp.dot(both, spread, preferred_element_type=F32))
    hot_ref[...] = sum(pieces[1:], pieces[0]).astype(BF16)
    divisor = jnp.maximum(count, 1).astype(F32)
    divisor_ref[...] = jnp.broadcast_to(divisor, (LANES, n)).T


def cold_sum_kernel(weight_ref, rows_ref, out_ref):
    out_ref[...] = jnp.dot(weight_ref[...], rows_ref[...], preferred_element_type=F32)


def layer_kernel(part_ref, weight_ref, rows_ref, divisor_ref, w_self_ref, w_nbr_ref, bias_ref, out_ref):
    n = out_ref.shape[0]
    total = part_ref[...] + jnp.dot(weight_ref[...], rows_ref[...], preferred_element_type=F32)
    own = total[:n].astype(BF16)
    divisor = jnp.concatenate([divisor_ref[...]] * (D // LANES), axis=1)
    mean = (total[n:] / divisor).astype(BF16)
    mixed = jnp.dot(own, w_self_ref[...], preferred_element_type=F32)
    mixed = mixed + jnp.dot(mean, w_nbr_ref[...], preferred_element_type=F32) + bias_ref[...]
    out_ref[...] = jnp.maximum(mixed, 0.0).astype(BF16)


def device_at(owner, z, core):
    return owner * 32 + (z % 16) * 2 + core


def home(owner):
    return (owner // 8) * 2 + owner % 2


def shifted(array, starts, step):
    pairs = [
        (device_at(o, home(o) + s, c), device_at(o, home(o) + s + step, c))
        for o in range(32)
        for s in starts
        for c in range(2)
    ]
    return lax.ppermute(array, ("owner", "replica"), pairs)


def other_core(array):
    return lax.ppermute(array, ("owner", "replica"), [(i, i ^ 1) for i in range(1024)])


def per_device(
    cold_vals,
    cold_scales,
    hot_vals,
    hot_scales,
    cold_req,
    hot_holder,
    hot_slot,
    self_pos,
    nbr_pos,
    nbr_count,
    w_self,
    w_nbr,
    bias,
):
    owner = lax.axis_index("owner")
    replica = lax.axis_index("replica")
    core = replica % 2
    steps = (replica // 2 - home(owner)) % 16

    own = dequantize(hot_vals, hot_scales)
    ask, place = call(
        ask_kernel,
        [jax.ShapeDtypeStruct((32, 1, LANES), I32), jax.ShapeDtypeStruct((256, LANES), I32)],
        [core.reshape(1), cold_req.reshape(1, 1024), hot_holder.reshape(1, 256), hot_slot.reshape(1, 256)],
        scalars=1,
    )
    up = jnp.where(steps == 0, own, 0)
    down = jnp.where(steps == 8, own, 0)
    up = up + shifted(own, (0,), 8)
    down = down + shifted(own, (8,), -8)

    asked = lax.all_to_all(ask, "owner", split_axis=0, concat_axis=0, tiled=True)
    table = dequantize(cold_vals, cold_scales)
    asked, up, down = lax.optimization_barrier((asked, up, down))
    served = call(
        serve_cold_kernel,
        jax.ShapeDtypeStruct((1024, D), BF16),
        [asked, table],
        vmem=24,
        flops=2 * 1024 * 2048 * D,
        moved=5 * MIB,
    )
    cold_rows = lax.all_to_all(served.reshape(32, 32, D), "owner", split_axis=0, concat_axis=0, tiled=True)

    for step, starts in ((4, (0, 8)), (2, (0, 4, 8, 12)), (1, (0, 2, 4, 6, 8, 10, 12, 14))):
        from_below, from_above = shifted(up, starts, step), shifted(down, starts, -step)
        up, down = up + from_below, down + from_above
    up2, down2 = other_core(up), other_core(down)
    hot_served = call(
        serve_hot_kernel,
        jax.ShapeDtypeStruct((512, D), BF16),
        [((owner % 8) // 2).reshape(1), asked, up, up2, down, down2],
        scalars=1,
        flops=2 * 512 * 128 * D,
        moved=2 * MIB,
    )

    weight_cold, weight_hot, divisor = call(
        weigh_kernel,
        [
            jax.ShapeDtypeStruct((512, 1024), BF16),
            jax.ShapeDtypeStruct((512, 512), BF16),
            jax.ShapeDtypeStruct((256, LANES), F32),
        ],
        [
            self_pos.reshape(1, 256),
            jnp.transpose(nbr_pos.reshape(256, F)).reshape(F, 1, 256),
            nbr_count.reshape(1, 256),
            place,
        ],
        flops=16 * 512 * 1280,
        moved=2 * MIB,
    )

    hot_served, cold_rows = lax.optimization_barrier((hot_served, cold_rows))
    groups = [[x * 8 + 2 * pair + b for x in range(4) for b in range(2)] for pair in range(4)]
    hot_rows = lax.all_to_all(
        hot_served.reshape(8, 64, D), "owner", split_axis=0, concat_axis=0, tiled=True, axis_index_groups=groups
    )
    part = call(
        cold_sum_kernel,
        jax.ShapeDtypeStruct((512, D), F32),
        [weight_cold, cold_rows.reshape(1024, D)],
        flops=2 * 512 * 1024 * D,
        moved=4 * MIB,
    )
    hidden = call(
        layer_kernel,
        jax.ShapeDtypeStruct((256, 1024), BF16),
        [part, weight_hot, hot_rows.reshape(512, D), divisor, w_self, w_nbr, bias.reshape(1, 1024)],
        vmem=24,
        flops=2 * 512 * 512 * D + 4 * 256 * D * 1024,
        moved=6 * MIB,
    )
    return hidden.reshape(1, 1, 256, 1024)


def solution(mesh):
    return jax.shard_map(
        per_device,
        mesh=mesh,
        in_specs=(
            P("owner", None),
            P("owner", None),
            P("replica", None),
            P("replica", None),
            P("owner", "replica", None),
            P("owner", "replica", None, None),
            P("owner", "replica", None),
            P("owner", "replica", None),
            P("owner", "replica", None, None),
            P("owner", "replica", None),
            P(),
            P(),
            P(),
        ),
        out_specs=P("owner", "replica", None, None),
        check_vma=False,
    )
```

```python
import jax
import jax.numpy as jnp
from jax import lax
from jax.experimental import pallas as pl
from jax.experimental.pallas import tpu as pltpu
from jax.sharding import PartitionSpec as P

D = 768
F = 15
SB = 128
NB = 6
CAP = 32
HCAP = 16
FAR = (4, 12, 8)
LANES = 128
MIB = 1024 * 1024
F32 = jnp.float32
BF16 = jnp.bfloat16
I32 = jnp.int32


def iota(shape, axis):
    return lax.broadcasted_iota(I32, shape, axis)


def call(body, outs, ins, scalars=0, away=0, scratch=(), vmem=16, flops=0, moved=0):
    smem = pl.BlockSpec(memory_space=pltpu.SMEM)
    full = pl.BlockSpec(memory_space=pltpu.VMEM)
    hbm = pl.BlockSpec(memory_space=pltpu.HBM)
    many = isinstance(outs, (list, tuple))
    return pl.pallas_call(
        body,
        out_shape=outs,
        in_specs=[smem] * scalars + [hbm] * away + [full] * (len(ins) - scalars - away),
        out_specs=[full] * len(outs) if many else full,
        scratch_shapes=list(scratch),
        compiler_params=pltpu.CompilerParams(vmem_limit_bytes=vmem * MIB),
        cost_estimate=pl.CostEstimate(flops=flops, bytes_accessed=moved, transcendentals=0),
    )(*ins)


def fetch(pairs, sems):
    copies = [pltpu.make_async_copy(src, dst, sems.at[i]) for i, (src, dst) in enumerate(pairs)]
    for copy in copies:
        copy.start()
    return copies


def scale_terms(across):
    blank = jnp.zeros((8 - NB, LANES), F32)
    terms = []
    for _ in range(3):
        term = across.astype(BF16).astype(F32)
        across = across - term
        terms += [term, blank]
    terms.append(jnp.zeros((LANES - 24, LANES), F32))
    return jnp.concatenate(terms, axis=0).T.astype(BF16)


def dequantize_kernel(vals_ref, scales_ref, out_ref):
    term, feature = iota((LANES, D), 0), iota((LANES, D), 1)
    widen = ((term % 8 == feature // SB) & (term < 24)).astype(F32).astype(BF16)
    terms = [scale_terms(scales_ref[:, at : at + LANES]) for at in range(0, vals_ref.shape[0], LANES)]
    scales = jnp.dot(jnp.concatenate(terms, axis=0), widen, preferred_element_type=F32)
    out_ref[...] = (vals_ref[...].astype(F32) * scales).astype(BF16)


def dequantize(vals, scales):
    rows = vals.shape[0]
    return call(
        dequantize_kernel,
        jax.ShapeDtypeStruct((rows, D), BF16),
        [vals, scales.T],
        vmem=12,
        flops=rows * D,
        moved=rows * D * 4,
    )


def ask_kernel(cold_hbm, holder_hbm, slot_hbm, ask_ref, place_ref, cold_ref, holder_ref, slot_ref, sems):
    copies = fetch([(holder_hbm, holder_ref), (slot_hbm, slot_ref), (cold_hbm, cold_ref)], sems)
    for copy in copies:
        copy.wait()
    n = holder_ref.shape[1]
    across = jnp.broadcast_to(holder_ref[...], (n, n))
    down = across.T
    earlier = (across == down) & (iota((n, n), 1) < iota((n, n), 0))
    rank = jnp.sum(earlier.astype(F32), axis=1, keepdims=True).astype(I32)
    place_ref[...] = down[:, :LANES] * HCAP + rank
    owners = ask_ref.shape[0]
    named = jnp.broadcast_to(holder_ref[...], (owners, n)) == iota((owners, n), 0)
    slots = jnp.broadcast_to(slot_ref[...], (owners, n)).astype(F32)
    left = jnp.where(named, slots, 0.0).astype(BF16)
    right = (rank + CAP == iota((n, LANES), 1)).astype(F32).astype(BF16)
    hot = jnp.dot(left, right, preferred_element_type=F32).astype(I32)
    column = iota((1, LANES), 1)
    for p in range(owners):
        cold = cold_ref[:, (p // 4) * LANES : (p // 4 + 1) * LANES]
        if p % 4:
            cold = pltpu.roll(cold, LANES - CAP * (p % 4), 1)
        ask_ref[p] = jnp.where(column < CAP, cold, hot[p : p + 1])


def transposed(rows):
    n = rows.shape[0]
    if n < LANES:
        rows = jnp.concatenate([rows, jnp.zeros((LANES - n, LANES), I32)], axis=0)
    return rows.T


def pick(asks, first, group, at, count, source):
    rows = source.shape[0]
    return jnp.concatenate(
        [
            (asks[at : at + count, p : p + 1] == iota((count, rows), 1)).astype(F32).astype(BF16)
            for p in range(first, first + group)
        ],
        axis=0,
    )


def serve_cold_kernel(asked_ref, table_ref, out_ref):
    asks = transposed(jnp.concatenate([asked_ref[p] for p in range(32)], axis=0))
    group = 8
    for first in range(0, 32, group):
        mask = pick(asks, first, group, 0, CAP, table_ref)
        out_ref[first * CAP : (first + group) * CAP, :] = jnp.dot(
            mask, table_ref[...], preferred_element_type=F32
        ).astype(BF16)


def serve_hot_kernel(asked_ref, held_ref, out_ref):
    asks = transposed(jnp.concatenate([asked_ref[p] for p in range(32)], axis=0))
    mask = pick(asks, 0, 32, CAP, HCAP, held_ref)
    out_ref[...] = jnp.dot(mask, held_ref[...], preferred_element_type=F32).astype(BF16)


def weigh_kernel(self_ref, nbr_ref, count_ref, place_ref, cold_ref, hot_ref, divisor_ref):
    n = self_ref.shape[1]
    count = count_ref[...]
    own = self_ref[...]
    live = [jnp.where(count > f, nbr_ref[f], -1) for f in range(F)]

    def weights(at):
        position = iota((LANES, n), 0) + at * LANES
        picked = (own == position).astype(F32)
        times = jnp.zeros((LANES, n), F32)
        for f in range(F):
            times = times + (live[f] == position).astype(F32)
        return jnp.concatenate([picked.T, times.T], axis=0).astype(BF16)

    n_cold, slots = cold_ref.shape[1] // LANES, hot_ref.shape[1]
    for at in range(n_cold):
        cold_ref[:, at * LANES : (at + 1) * LANES] = weights(at)
    n_hot = place_ref.shape[0]
    hot = jnp.concatenate([weights(n_cold + at) for at in range(n_hot // LANES)], axis=1)
    place = jnp.concatenate([place_ref[...]] * (slots // LANES), axis=1)
    spread = (place == iota((n_hot, slots), 1)).astype(F32).astype(BF16)
    hot_ref[...] = jnp.dot(hot, spread, preferred_element_type=F32).astype(BF16)
    divisor = jnp.maximum(count, 1).astype(F32)
    divisor_ref[...] = jnp.broadcast_to(divisor, (LANES, n)).T


def cold_sum_kernel(w_self_hbm, w_nbr_hbm, weight_ref, rows_ref, weight_hot_ref, out_ref, w_ref, kept_ref, sems):
    copies = fetch([(w_self_hbm, w_ref.at[pl.ds(0, D)]), (w_nbr_hbm, w_ref.at[pl.ds(D, D)])], sems)
    out_ref[...] = jnp.dot(weight_ref[...], rows_ref[...], preferred_element_type=F32)
    kept_ref[...] = weight_hot_ref[...]
    for copy in copies:
        copy.wait()


def layer_kernel(part_ref, weight_ref, rows_ref, divisor_ref, w_ref, bias_ref, out_ref):
    n = out_ref.shape[0]
    total = part_ref[...] + jnp.dot(weight_ref[...], rows_ref[...], preferred_element_type=F32)
    own = total[:n].astype(BF16)
    divisor = jnp.concatenate([divisor_ref[...]] * (D // LANES), axis=1)
    mean = (total[n:] / divisor).astype(BF16)
    both = jnp.concatenate([own, mean], axis=1)
    mixed = jnp.dot(both, w_ref[...], preferred_element_type=F32) + bias_ref[...]
    out_ref[...] = jnp.maximum(mixed, 0.0).astype(BF16)


def send(array, starts, step):
    pairs = [
        (o * 32 + (o // 2 + s) % 16 * 2 + o % 2, o * 32 + (o // 2 + s + step) % 16 * 2 + o % 2)
        for o in range(32)
        for s in starts
    ]
    return lax.ppermute(array, ("owner", "replica"), pairs)


def across_chip(array):
    pairs = [(o * 32 + z * 2 + o % 2, o * 32 + z * 2 + 1 - o % 2) for o in range(32) for z in range(16)]
    return lax.ppermute(array, ("owner", "replica"), pairs)


def per_device(
    cold_vals,
    cold_scales,
    hot_vals,
    hot_scales,
    cold_req,
    hot_holder,
    hot_slot,
    self_pos,
    nbr_pos,
    nbr_count,
    w_self,
    w_nbr,
    bias,
):
    owner = lax.axis_index("owner")
    replica = lax.axis_index("replica")

    ask, place = call(
        ask_kernel,
        [jax.ShapeDtypeStruct((32, 1, LANES), I32), jax.ShapeDtypeStruct((256, LANES), I32)],
        [cold_req.reshape(1, 1024), hot_holder.reshape(1, 256), hot_slot.reshape(1, 256)],
        away=3,
        scratch=[
            pltpu.VMEM((1, 1024), I32),
            pltpu.VMEM((1, 256), I32),
            pltpu.VMEM((1, 256), I32),
            pltpu.SemaphoreType.DMA((3,)),
        ],
        vmem=60,
    )
    asked = lax.all_to_all(ask, "owner", split_axis=0, concat_axis=0, tiled=True)
    own = dequantize(hot_vals, hot_scales)
    asked, own = lax.optimization_barrier((asked, own))
    table = dequantize(cold_vals, cold_scales)
    served = call(
        serve_cold_kernel,
        jax.ShapeDtypeStruct((1024, D), BF16),
        [asked, table],
        vmem=12,
        flops=2 * 1024 * 2048 * D,
        moved=5 * MIB,
    )
    cold_rows = lax.all_to_all(served.reshape(32, CAP, D), "owner", split_axis=0, concat_axis=0, tiled=True)

    far = [send(own, (0,), step) for step in FAR]
    steps = (replica // 2 - owner // 2) % 16
    rows = jnp.where(steps == 0, own, sum(far[1:], far[0]))
    near = [send(rows, (0, *FAR), step) for step in (1, 15, 2)]
    rows = jnp.where(steps % 4 == 0, rows, sum(near[1:], near[0]))
    held = jnp.where(replica % 2 == owner % 2, rows, across_chip(rows))
    hot_served = call(
        serve_hot_kernel,
        jax.ShapeDtypeStruct((512, D), BF16),
        [asked, held],
        vmem=4,
        flops=2 * 512 * 128 * D,
        moved=2 * MIB,
    )
    hot_served, cold_rows = lax.optimization_barrier((hot_served, cold_rows))
    hot_rows = lax.all_to_all(hot_served.reshape(32, HCAP, D), "owner", split_axis=0, concat_axis=0, tiled=True)

    weight_cold, weight_hot, divisor = call(
        weigh_kernel,
        [
            jax.ShapeDtypeStruct((512, 1024), BF16),
            jax.ShapeDtypeStruct((512, 512), BF16),
            jax.ShapeDtypeStruct((256, LANES), F32),
        ],
        [
            self_pos.reshape(1, 256),
            jnp.transpose(nbr_pos.reshape(256, F)).reshape(F, 1, 256),
            nbr_count.reshape(1, 256),
            place,
        ],
        vmem=6,
        flops=16 * 512 * 1280,
        moved=2 * MIB,
    )
    part, weights, weight_hot = call(
        cold_sum_kernel,
        [
            jax.ShapeDtypeStruct((512, D), F32),
            jax.ShapeDtypeStruct((2 * D, 1024), BF16),
            jax.ShapeDtypeStruct((512, 512), BF16),
        ],
        [w_self, w_nbr, weight_cold, cold_rows.reshape(1024, D), weight_hot],
        away=2,
        scratch=[pltpu.SemaphoreType.DMA((2,))],
        vmem=6,
        flops=2 * 512 * 1024 * D,
        moved=8 * MIB,
    )
    hidden = call(
        layer_kernel,
        jax.ShapeDtypeStruct((256, 1024), BF16),
        [part, weight_hot, hot_rows.reshape(512, D), divisor, weights, bias.reshape(1, 1024)],
        vmem=8,
        flops=2 * 512 * 512 * D + 4 * 256 * D * 1024,
        moved=8 * MIB,
    )
    return hidden.reshape(1, 1, 256, 1024)


def solution(mesh):
    return jax.shard_map(
        per_device,
        mesh=mesh,
        in_specs=(
            P("owner", None),
            P("owner", None),
            P("replica", None),
            P("replica", None),
            P("owner", "replica", None),
            P("owner", "replica", None, None),
            P("owner", "replica", None),
            P("owner", "replica", None),
            P("owner", "replica", None, None),
            P("owner", "replica", None),
            P(),
            P(),
            P(),
        ),
        out_specs=P("owner", "replica", None, None),
        check_vma=False,
    )
```

```python
import jax
import jax.numpy as jnp
from jax import lax
from jax.experimental import pallas as pl
from jax.experimental.pallas import tpu as pltpu
from jax.sharding import PartitionSpec as P

D = 768
F = 15
SB = 128
NB = 6
CAP = 32
HCAP = 16
LANES = 128
MIB = 1024 * 1024
F32 = jnp.float32
BF16 = jnp.bfloat16
I32 = jnp.int32


def iota(shape, axis):
    return lax.broadcasted_iota(I32, shape, axis)


def call(body, outs, ins, scalars=0, away=0, scratch=(), vmem=16, flops=0, moved=0):
    smem = pl.BlockSpec(memory_space=pltpu.SMEM)
    full = pl.BlockSpec(memory_space=pltpu.VMEM)
    hbm = pl.BlockSpec(memory_space=pltpu.HBM)
    many = isinstance(outs, (list, tuple))
    return pl.pallas_call(
        body,
        out_shape=outs,
        in_specs=[smem] * scalars + [hbm] * away + [full] * (len(ins) - scalars - away),
        out_specs=[full] * len(outs) if many else full,
        scratch_shapes=list(scratch),
        compiler_params=pltpu.CompilerParams(vmem_limit_bytes=vmem * MIB),
        cost_estimate=pl.CostEstimate(flops=flops, bytes_accessed=moved, transcendentals=0),
    )(*ins)


def fetch(pairs, sems):
    copies = [pltpu.make_async_copy(src, dst, sems.at[i]) for i, (src, dst) in enumerate(pairs)]
    for copy in copies:
        copy.start()
    return copies


def scale_terms(across):
    blank = jnp.zeros((8 - NB, LANES), F32)
    terms = []
    for _ in range(3):
        term = across.astype(BF16).astype(F32)
        across = across - term
        terms += [term, blank]
    terms.append(jnp.zeros((LANES - 24, LANES), F32))
    return jnp.concatenate(terms, axis=0).T.astype(BF16)


def dequantize_kernel(vals_ref, scales_ref, out_ref):
    term, feature = iota((LANES, D), 0), iota((LANES, D), 1)
    widen = ((term % 8 == feature // SB) & (term < 24)).astype(F32).astype(BF16)
    terms = [scale_terms(scales_ref[:, at : at + LANES]) for at in range(0, vals_ref.shape[0], LANES)]
    scales = jnp.dot(jnp.concatenate(terms, axis=0), widen, preferred_element_type=F32)
    out_ref[...] = (vals_ref[...].astype(F32) * scales).astype(BF16)


def dequantize(vals, scales):
    rows = vals.shape[0]
    return call(
        dequantize_kernel,
        jax.ShapeDtypeStruct((rows, D), BF16),
        [vals, scales.T],
        vmem=12,
        flops=rows * D,
        moved=rows * D * 4,
    )


def ask_kernel(cold_hbm, holder_hbm, slot_hbm, ask_ref, place_ref, cold_ref, holder_ref, slot_ref, sems):
    copies = fetch([(holder_hbm, holder_ref), (slot_hbm, slot_ref), (cold_hbm, cold_ref)], sems)
    for copy in copies:
        copy.wait()
    n = holder_ref.shape[1]
    across = jnp.broadcast_to(holder_ref[...], (n, n))
    down = across.T
    earlier = (across == down) & (iota((n, n), 1) < iota((n, n), 0))
    rank = jnp.sum(earlier.astype(F32), axis=1, keepdims=True).astype(I32)
    place_ref[...] = down[:, :LANES] * HCAP + rank
    owners = ask_ref.shape[0]
    named = jnp.broadcast_to(holder_ref[...], (owners, n)) == iota((owners, n), 0)
    slots = jnp.broadcast_to(slot_ref[...], (owners, n)).astype(F32)
    left = jnp.where(named, slots, 0.0).astype(BF16)
    right = (rank + CAP == iota((n, LANES), 1)).astype(F32).astype(BF16)
    hot = jnp.dot(left, right, preferred_element_type=F32).astype(I32)
    column = iota((1, LANES), 1)
    for p in range(owners):
        cold = cold_ref[:, (p // 4) * LANES : (p // 4 + 1) * LANES]
        if p % 4:
            cold = pltpu.roll(cold, LANES - CAP * (p % 4), 1)
        ask_ref[p] = jnp.where(column < CAP, cold, hot[p : p + 1])


def transposed(rows):
    n = rows.shape[0]
    if n < LANES:
        rows = jnp.concatenate([rows, jnp.zeros((LANES - n, LANES), I32)], axis=0)
    return rows.T


def pick(asks, first, group, at, count, source):
    rows = source.shape[0]
    return jnp.concatenate(
        [
            (asks[at : at + count, p : p + 1] == iota((count, rows), 1)).astype(F32).astype(BF16)
            for p in range(first, first + group)
        ],
        axis=0,
    )


def serve_cold_kernel(asked_ref, table_ref, out_ref):
    asks = transposed(jnp.concatenate([asked_ref[p] for p in range(32)], axis=0))
    group = 8
    for first in range(0, 32, group):
        mask = pick(asks, first, group, 0, CAP, table_ref)
        out_ref[first * CAP : (first + group) * CAP, :] = jnp.dot(
            mask, table_ref[...], preferred_element_type=F32
        ).astype(BF16)


def serve_hot_kernel(asked_ref, held_ref, out_ref):
    asks = transposed(jnp.concatenate([asked_ref[p] for p in range(32)], axis=0))
    mask = pick(asks, 0, 32, CAP, HCAP, held_ref)
    out_ref[...] = jnp.dot(mask, held_ref[...], preferred_element_type=F32).astype(BF16)


def weigh_kernel(self_ref, nbr_ref, count_ref, place_ref, cold_ref, hot_ref, divisor_ref):
    n = self_ref.shape[1]
    count = count_ref[...]
    own = self_ref[...]
    live = [jnp.where(count > f, nbr_ref[f], -1) for f in range(F)]

    def weights(at):
        position = iota((LANES, n), 0) + at * LANES
        picked = (own == position).astype(F32)
        times = jnp.zeros((LANES, n), F32)
        for f in range(F):
            times = times + (live[f] == position).astype(F32)
        return jnp.concatenate([picked.T, times.T], axis=0).astype(BF16)

    n_cold, slots = cold_ref.shape[1] // LANES, hot_ref.shape[1]
    for at in range(n_cold):
        cold_ref[:, at * LANES : (at + 1) * LANES] = weights(at)
    n_hot = place_ref.shape[0]
    hot = jnp.concatenate([weights(n_cold + at) for at in range(n_hot // LANES)], axis=1)
    place = jnp.concatenate([place_ref[...]] * (slots // LANES), axis=1)
    spread = (place == iota((n_hot, slots), 1)).astype(F32).astype(BF16)
    hot_ref[...] = jnp.dot(hot, spread, preferred_element_type=F32).astype(BF16)
    divisor = jnp.maximum(count, 1).astype(F32)
    divisor_ref[...] = jnp.broadcast_to(divisor, (LANES, n)).T


def cold_sum_kernel(w_self_hbm, w_nbr_hbm, weight_ref, rows_ref, weight_hot_ref, out_ref, w_ref, kept_ref, sems):
    copies = fetch([(w_self_hbm, w_ref.at[pl.ds(0, D)]), (w_nbr_hbm, w_ref.at[pl.ds(D, D)])], sems)
    out_ref[...] = jnp.dot(weight_ref[...], rows_ref[...], preferred_element_type=F32)
    kept_ref[...] = weight_hot_ref[...]
    for copy in copies:
        copy.wait()


def layer_kernel(part_ref, weight_ref, rows_ref, divisor_ref, w_ref, bias_ref, out_ref):
    n = out_ref.shape[0]
    total = part_ref[...] + jnp.dot(weight_ref[...], rows_ref[...], preferred_element_type=F32)
    own = total[:n].astype(BF16)
    divisor = jnp.concatenate([divisor_ref[...]] * (D // LANES), axis=1)
    mean = (total[n:] / divisor).astype(BF16)
    both = jnp.concatenate([own, mean], axis=1)
    mixed = jnp.dot(both, w_ref[...], preferred_element_type=F32) + bias_ref[...]
    out_ref[...] = jnp.maximum(mixed, 0.0).astype(BF16)


def relays(home):
    place = min(home % 4, 2)
    return [b * 4 + place for b in range(4) if b != home // 4]


def onward(z):
    steps = {0: (1, 2, -1), 1: (-1, 1, 2), 2: (-2, -1, 1), 3: (-3, -2, -1)}
    return [(z + step) % 16 for step in steps[z % 4]]


def down_columns(array, edges):
    pairs = [
        (o * 32 + z * 2 + o % 2, o * 32 + there * 2 + o % 2) for o in range(32) for z, there in edges(o // 2)
    ]
    return lax.ppermute(array, ("owner", "replica"), pairs)


def across_chip(array):
    pairs = [(o * 32 + z * 2 + o % 2, o * 32 + z * 2 + 1 - o % 2) for o in range(32) for z in range(16)]
    return lax.ppermute(array, ("owner", "replica"), pairs)


def per_device(
    cold_vals,
    cold_scales,
    hot_vals,
    hot_scales,
    cold_req,
    hot_holder,
    hot_slot,
    self_pos,
    nbr_pos,
    nbr_count,
    w_self,
    w_nbr,
    bias,
):
    owner = lax.axis_index("owner")
    replica = lax.axis_index("replica")

    ask, place = call(
        ask_kernel,
        [jax.ShapeDtypeStruct((32, 1, LANES), I32), jax.ShapeDtypeStruct((256, LANES), I32)],
        [cold_req.reshape(1, 1024), hot_holder.reshape(1, 256), hot_slot.reshape(1, 256)],
        away=3,
        scratch=[
            pltpu.VMEM((1, 1024), I32),
            pltpu.VMEM((1, 256), I32),
            pltpu.VMEM((1, 256), I32),
            pltpu.SemaphoreType.DMA((3,)),
        ],
        vmem=60,
    )
    asked = lax.all_to_all(ask, "owner", split_axis=0, concat_axis=0, tiled=True)
    own = dequantize(hot_vals, hot_scales)
    asked, own = lax.optimization_barrier((asked, own))
    table = dequantize(cold_vals, cold_scales)
    served = call(
        serve_cold_kernel,
        jax.ShapeDtypeStruct((1024, D), BF16),
        [asked, table],
        vmem=12,
        flops=2 * 1024 * 2048 * D,
        moved=5 * MIB,
    )
    cold_rows = lax.all_to_all(served.reshape(32, CAP, D), "owner", split_axis=0, concat_axis=0, tiled=True)

    z, home = replica // 2, owner // 2
    far = [down_columns(own, lambda h, turn=turn: [(h, relays(h)[turn])]) for turn in (2, 1, 0)]
    rows = jnp.where(z == home, own, far[0] + far[1] + far[2])
    beside = [down_columns(own, lambda h, turn=turn: [(h, onward(h)[turn])]) for turn in range(3)]
    near = [
        down_columns(rows, lambda h, turn=turn: [(at, onward(at)[turn]) for at in relays(h)]) for turn in range(3)
    ]
    relay = (z == home) | ((z // 4 != home // 4) & (z % 4 == jnp.minimum(home % 4, 2)))
    rows = jnp.where(relay, rows, sum(beside[1:] + near, beside[0]))
    held = jnp.where(replica % 2 == owner % 2, rows, across_chip(rows))
    hot_served = call(
        serve_hot_kernel,
        jax.ShapeDtypeStruct((512, D), BF16),
        [asked, held],
        vmem=4,
        flops=2 * 512 * 128 * D,
        moved=2 * MIB,
    )
    hot_served, cold_rows = lax.optimization_barrier((hot_served, cold_rows))
    hot_rows = lax.all_to_all(hot_served.reshape(32, HCAP, D), "owner", split_axis=0, concat_axis=0, tiled=True)

    weight_cold, weight_hot, divisor = call(
        weigh_kernel,
        [
            jax.ShapeDtypeStruct((512, 1024), BF16),
            jax.ShapeDtypeStruct((512, 512), BF16),
            jax.ShapeDtypeStruct((256, LANES), F32),
        ],
        [
            self_pos.reshape(1, 256),
            jnp.transpose(nbr_pos.reshape(256, F)).reshape(F, 1, 256),
            nbr_count.reshape(1, 256),
            place,
        ],
        vmem=6,
        flops=16 * 512 * 1280,
        moved=2 * MIB,
    )
    part, weights, weight_hot = call(
        cold_sum_kernel,
        [
            jax.ShapeDtypeStruct((512, D), F32),
            jax.ShapeDtypeStruct((2 * D, 1024), BF16),
            jax.ShapeDtypeStruct((512, 512), BF16),
        ],
        [w_self, w_nbr, weight_cold, cold_rows.reshape(1024, D), weight_hot],
        away=2,
        scratch=[pltpu.SemaphoreType.DMA((2,))],
        vmem=6,
        flops=2 * 512 * 1024 * D,
        moved=8 * MIB,
    )
    hidden = call(
        layer_kernel,
        jax.ShapeDtypeStruct((256, 1024), BF16),
        [part, weight_hot, hot_rows.reshape(512, D), divisor, weights, bias.reshape(1, 1024)],
        vmem=8,
        flops=2 * 512 * 512 * D + 4 * 256 * D * 1024,
        moved=8 * MIB,
    )
    return hidden.reshape(1, 1, 256, 1024)


def solution(mesh):
    return jax.shard_map(
        per_device,
        mesh=mesh,
        in_specs=(
            P("owner", None),
            P("owner", None),
            P("replica", None),
            P("replica", None),
            P("owner", "replica", None),
            P("owner", "replica", None, None),
            P("owner", "replica", None),
            P("owner", "replica", None),
            P("owner", "replica", None, None),
            P("owner", "replica", None),
            P(),
            P(),
            P(),
        ),
        out_specs=P("owner", "replica", None, None),
        check_vma=False,
    )
```

```python
import jax
import jax.numpy as jnp
from jax import lax
from jax.experimental import pallas as pl
from jax.experimental.pallas import tpu as pltpu
from jax.sharding import PartitionSpec as P

D = 768
F = 15
SB = 128
NB = 6
CAP = 32
HCAP = 16
LANES = 128
MIB = 1024 * 1024
F32 = jnp.float32
BF16 = jnp.bfloat16
I32 = jnp.int32


def iota(shape, axis):
    return lax.broadcasted_iota(I32, shape, axis)


def call(body, outs, ins, scalars=0, away=0, scratch=(), vmem=16, flops=0, moved=0):
    smem = pl.BlockSpec(memory_space=pltpu.SMEM)
    full = pl.BlockSpec(memory_space=pltpu.VMEM)
    hbm = pl.BlockSpec(memory_space=pltpu.HBM)
    many = isinstance(outs, (list, tuple))
    return pl.pallas_call(
        body,
        out_shape=outs,
        in_specs=[smem] * scalars + [hbm] * away + [full] * (len(ins) - scalars - away),
        out_specs=[full] * len(outs) if many else full,
        scratch_shapes=list(scratch),
        compiler_params=pltpu.CompilerParams(vmem_limit_bytes=vmem * MIB),
        cost_estimate=pl.CostEstimate(flops=flops, bytes_accessed=moved, transcendentals=0),
    )(*ins)


def fetch(pairs, sems):
    copies = [pltpu.make_async_copy(src, dst, sems.at[i]) for i, (src, dst) in enumerate(pairs)]
    for copy in copies:
        copy.start()
    return copies


def scale_terms(across):
    blank = jnp.zeros((8 - NB, LANES), F32)
    terms = []
    for _ in range(3):
        term = across.astype(BF16).astype(F32)
        across = across - term
        terms += [term, blank]
    terms.append(jnp.zeros((LANES - 24, LANES), F32))
    return jnp.concatenate(terms, axis=0).T.astype(BF16)


def dequantize_kernel(vals_ref, scales_ref, out_ref):
    term, feature = iota((LANES, D), 0), iota((LANES, D), 1)
    widen = ((term % 8 == feature // SB) & (term < 24)).astype(F32).astype(BF16)
    terms = [scale_terms(scales_ref[:, at : at + LANES]) for at in range(0, vals_ref.shape[0], LANES)]
    scales = jnp.dot(jnp.concatenate(terms, axis=0), widen, preferred_element_type=F32)
    out_ref[...] = (vals_ref[...].astype(F32) * scales).astype(BF16)


def dequantize(vals, scales):
    rows = vals.shape[0]
    return call(
        dequantize_kernel,
        jax.ShapeDtypeStruct((rows, D), BF16),
        [vals, scales.T],
        vmem=12,
        flops=rows * D,
        moved=rows * D * 4,
    )


def ask_kernel(cold_hbm, holder_hbm, slot_hbm, ask_ref, place_ref, cold_ref, holder_ref, slot_ref, sems):
    copies = fetch([(holder_hbm, holder_ref), (slot_hbm, slot_ref), (cold_hbm, cold_ref)], sems)
    for copy in copies:
        copy.wait()
    n = holder_ref.shape[1]
    across = jnp.broadcast_to(holder_ref[...], (n, n))
    down = across.T
    earlier = (across == down) & (iota((n, n), 1) < iota((n, n), 0))
    rank = jnp.sum(earlier.astype(F32), axis=1, keepdims=True).astype(I32)
    place_ref[...] = down[:, :LANES] * HCAP + rank
    owners = ask_ref.shape[0]
    named = jnp.broadcast_to(holder_ref[...], (owners, n)) == iota((owners, n), 0)
    slots = jnp.broadcast_to(slot_ref[...], (owners, n)).astype(F32)
    left = jnp.where(named, slots, 0.0).astype(BF16)
    right = (rank + CAP == iota((n, LANES), 1)).astype(F32).astype(BF16)
    hot = jnp.dot(left, right, preferred_element_type=F32).astype(I32)
    column = iota((1, LANES), 1)
    for p in range(owners):
        cold = cold_ref[:, (p // 4) * LANES : (p // 4 + 1) * LANES]
        if p % 4:
            cold = pltpu.roll(cold, LANES - CAP * (p % 4), 1)
        ask_ref[p] = jnp.where(column < CAP, cold, hot[p : p + 1])


def transposed(rows):
    n = rows.shape[0]
    if n < LANES:
        rows = jnp.concatenate([rows, jnp.zeros((LANES - n, LANES), I32)], axis=0)
    return rows.T


def pick(asks, first, group, at, count, source):
    rows = source.shape[0]
    return jnp.concatenate(
        [
            (asks[at : at + count, p : p + 1] == iota((count, rows), 1)).astype(F32).astype(BF16)
            for p in range(first, first + group)
        ],
        axis=0,
    )


def serve_cold_kernel(asked_ref, table_ref, out_ref):
    asks = transposed(jnp.concatenate([asked_ref[p] for p in range(32)], axis=0))
    group = 8
    for first in range(0, 32, group):
        mask = pick(asks, first, group, 0, CAP, table_ref)
        out_ref[first * CAP : (first + group) * CAP, :] = jnp.dot(
            mask, table_ref[...], preferred_element_type=F32
        ).astype(BF16)


def serve_hot_kernel(asked_ref, held_ref, out_ref):
    asks = transposed(jnp.concatenate([asked_ref[p] for p in range(32)], axis=0))
    mask = pick(asks, 0, 32, CAP, HCAP, held_ref)
    out_ref[...] = jnp.dot(mask, held_ref[...], preferred_element_type=F32).astype(BF16)


def weigh_kernel(self_ref, nbr_ref, count_ref, place_ref, cold_ref, hot_ref, divisor_ref):
    n = self_ref.shape[1]
    count = count_ref[...]
    own = self_ref[...]
    live = [jnp.where(count > f, nbr_ref[f], -1) for f in range(F)]

    def weights(at):
        position = iota((LANES, n), 0) + at * LANES
        picked = (own == position).astype(F32)
        times = jnp.zeros((LANES, n), F32)
        for f in range(F):
            times = times + (live[f] == position).astype(F32)
        return jnp.concatenate([picked.T, times.T], axis=0).astype(BF16)

    n_cold, slots = cold_ref.shape[1] // LANES, hot_ref.shape[1]
    for at in range(n_cold):
        cold_ref[:, at * LANES : (at + 1) * LANES] = weights(at)
    n_hot = place_ref.shape[0]
    hot = jnp.concatenate([weights(n_cold + at) for at in range(n_hot // LANES)], axis=1)
    place = jnp.concatenate([place_ref[...]] * (slots // LANES), axis=1)
    spread = (place == iota((n_hot, slots), 1)).astype(F32).astype(BF16)
    hot_ref[...] = jnp.dot(hot, spread, preferred_element_type=F32).astype(BF16)
    divisor = jnp.maximum(count, 1).astype(F32)
    divisor_ref[...] = jnp.broadcast_to(divisor, (LANES, n)).T


def cold_sum_kernel(w_self_hbm, w_nbr_hbm, weight_ref, rows_ref, weight_hot_ref, out_ref, w_ref, kept_ref, sems):
    copies = fetch([(w_self_hbm, w_ref.at[pl.ds(0, D)]), (w_nbr_hbm, w_ref.at[pl.ds(D, D)])], sems)
    out_ref[...] = jnp.dot(weight_ref[...], rows_ref[...], preferred_element_type=F32)
    kept_ref[...] = weight_hot_ref[...]
    for copy in copies:
        copy.wait()


def layer_kernel(part_ref, weight_ref, rows_ref, divisor_ref, w_ref, bias_ref, out_ref):
    n = out_ref.shape[0]
    total = part_ref[...] + jnp.dot(weight_ref[...], rows_ref[...], preferred_element_type=F32)
    own = total[:n].astype(BF16)
    divisor = jnp.concatenate([divisor_ref[...]] * (D // LANES), axis=1)
    mean = (total[n:] / divisor).astype(BF16)
    both = jnp.concatenate([own, mean], axis=1)
    mixed = jnp.dot(both, w_ref[...], preferred_element_type=F32) + bias_ref[...]
    out_ref[...] = jnp.maximum(mixed, 0.0).astype(BF16)


def relays(home):
    place = min(home % 4, 2)
    return [b * 4 + place for b in range(4) if b != home // 4]


def onward(z):
    steps = {0: (1, 2, -1), 1: (-1, 1, 2), 2: (-2, -1, 1), 3: (-3, -2, -1)}
    return [(z + step) % 16 for step in steps[z % 4]]


def down_columns(array, edges):
    pairs = [
        (o * 32 + z * 2 + o % 2, o * 32 + there * 2 + o % 2) for o in range(32) for z, there in edges(o // 2)
    ]
    return lax.ppermute(array, ("owner", "replica"), pairs)


def across_chip(array):
    pairs = [(o * 32 + z * 2 + o % 2, o * 32 + z * 2 + 1 - o % 2) for o in range(32) for z in range(16)]
    return lax.ppermute(array, ("owner", "replica"), pairs)


def per_device(
    cold_vals,
    cold_scales,
    hot_vals,
    hot_scales,
    cold_req,
    hot_holder,
    hot_slot,
    self_pos,
    nbr_pos,
    nbr_count,
    w_self,
    w_nbr,
    bias,
):
    owner = lax.axis_index("owner")
    replica = lax.axis_index("replica")

    ask, place = call(
        ask_kernel,
        [jax.ShapeDtypeStruct((32, 1, LANES), I32), jax.ShapeDtypeStruct((256, LANES), I32)],
        [cold_req.reshape(1, 1024), hot_holder.reshape(1, 256), hot_slot.reshape(1, 256)],
        away=3,
        scratch=[
            pltpu.VMEM((1, 1024), I32),
            pltpu.VMEM((1, 256), I32),
            pltpu.VMEM((1, 256), I32),
            pltpu.SemaphoreType.DMA((3,)),
        ],
        vmem=60,
    )
    asked = lax.all_to_all(ask, "owner", split_axis=0, concat_axis=0, tiled=True)
    own = dequantize(hot_vals, hot_scales)
    asked, own = lax.optimization_barrier((asked, own))
    table = dequantize(cold_vals, cold_scales)
    served = call(
        serve_cold_kernel,
        jax.ShapeDtypeStruct((1024, D), BF16),
        [asked, table],
        vmem=12,
        flops=2 * 1024 * 2048 * D,
        moved=5 * MIB,
    )
    cold_rows = lax.all_to_all(served.reshape(32, CAP, D), "owner", split_axis=0, concat_axis=0, tiled=True)

    z, home = replica // 2, owner // 2
    far = [down_columns(own, lambda h, turn=turn: [(h, relays(h)[turn])]) for turn in (2, 1, 0)]
    rows = jnp.where(z == home, own, far[0] + far[1] + far[2])
    beside = [down_columns(own, lambda h, turn=turn: [(h, onward(h)[turn])]) for turn in (2, 1, 0)]
    near = [
        down_columns(rows, lambda h, turn=turn: [(at, onward(at)[turn]) for at in relays(h)])
        for turn in (2, 1, 0)
    ]
    relay = (z == home) | ((z // 4 != home // 4) & (z % 4 == jnp.minimum(home % 4, 2)))
    rows = jnp.where(relay, rows, sum(beside[1:] + near, beside[0]))
    held = jnp.where(replica % 2 == owner % 2, rows, across_chip(rows))
    hot_served = call(
        serve_hot_kernel,
        jax.ShapeDtypeStruct((512, D), BF16),
        [asked, held],
        vmem=4,
        flops=2 * 512 * 128 * D,
        moved=2 * MIB,
    )
    hot_served, cold_rows = lax.optimization_barrier((hot_served, cold_rows))
    hot_rows = lax.all_to_all(hot_served.reshape(32, HCAP, D), "owner", split_axis=0, concat_axis=0, tiled=True)

    weight_cold, weight_hot, divisor = call(
        weigh_kernel,
        [
            jax.ShapeDtypeStruct((512, 1024), BF16),
            jax.ShapeDtypeStruct((512, 512), BF16),
            jax.ShapeDtypeStruct((256, LANES), F32),
        ],
        [
            self_pos.reshape(1, 256),
            jnp.transpose(nbr_pos.reshape(256, F)).reshape(F, 1, 256),
            nbr_count.reshape(1, 256),
            place,
        ],
        vmem=6,
        flops=16 * 512 * 1280,
        moved=2 * MIB,
    )
    part, weights, weight_hot = call(
        cold_sum_kernel,
        [
            jax.ShapeDtypeStruct((512, D), F32),
            jax.ShapeDtypeStruct((2 * D, 1024), BF16),
            jax.ShapeDtypeStruct((512, 512), BF16),
        ],
        [w_self, w_nbr, weight_cold, cold_rows.reshape(1024, D), weight_hot],
        away=2,
        scratch=[pltpu.SemaphoreType.DMA((2,))],
        vmem=6,
        flops=2 * 512 * 1024 * D,
        moved=8 * MIB,
    )
    hidden = call(
        layer_kernel,
        jax.ShapeDtypeStruct((256, 1024), BF16),
        [part, weight_hot, hot_rows.reshape(512, D), divisor, weights, bias.reshape(1, 1024)],
        vmem=8,
        flops=2 * 512 * 512 * D + 4 * 256 * D * 1024,
        moved=8 * MIB,
    )
    return hidden.reshape(1, 1, 256, 1024)


def solution(mesh):
    return jax.shard_map(
        per_device,
        mesh=mesh,
        in_specs=(
            P("owner", None),
            P("owner", None),
            P("replica", None),
            P("replica", None),
            P("owner", "replica", None),
            P("owner", "replica", None, None),
            P("owner", "replica", None),
            P("owner", "replica", None),
            P("owner", "replica", None, None),
            P("owner", "replica", None),
            P(),
            P(),
            P(),
        ),
        out_specs=P("owner", "replica", None, None),
        check_vma=False,
    )
```
